256 devices in a mesh: dp: 2 (over x_lo), row: 8 (over y, x_hi), col: 16 (over z, core).
Axes of the slice: x: 4 (x_hi: 2, x_lo: 2; x = x_hi * 2 + x_lo), y: 4, z: 8, core: 2. Of those that a mesh axis runs over, the one named last changes fastest.
Arguments:
- small_w: bfloat16 [4096, 4096], P('col', 'row'), may hold values from -0.09375 to 0.09375
- grow_a: bfloat16 [8192, 4096], P('row', 'col'), may hold values from -0.09375 to 0.09375
- grow_b: bfloat16 [8192, 4096], P('col', 'row'), may hold values from -0.09375 to 0.09375
- inputs: bfloat16 [1024, 8192], P('dp', 'col'), may hold values from -6 to 6
- cotangent: bfloat16 [1024, 8192], P('dp', 'row'), may hold values from -0.1875 to 0.1875
Outputs:
- outputs: bfloat16 [1024, 8192], P(('dp', 'col'), 'row')
- big_weight: bfloat16 [8192, 8192], P('row', 'col')
- grad_weight: bfloat16 [8192, 8192], P('row', 'col')
- grad_a: float32 [8192, 4096], P('row', ('dp', 'col'))
- grad_b: float32 [8192, 4096], P('col', ('dp', 'row'))
The draws below stay inside these ranges and needn't reach their ends.
All inputs are finite; a program needn't handle non-finite values.
Results may differ from the reference program's by a relative error of at most 0.035.
Values may be sent and summed in bfloat16 or wider, within the bound.
No kernel may reach another device: no remote copies, remote signals or barrier semaphores. Data moves between devices by JAX's collectives and lax.ppermute only.
A program may use at most 64 MiB of HBM per device.

```python
import jax
import jax.numpy as jnp
from jax import lax

BIG = 8192
SMALL = 4096
TOKENS = 1024
N_DP = 2
N_ROW = 8
N_COL = 16


def block_scale(key, shape, cuts, smallest, largest):
    def one(position, shards_of):
        draws = jax.random.uniform(jax.random.fold_in(jax.random.fold_in(key, 6), position), (shards_of,), jnp.float32, smallest / len(cuts), largest / len(cuts))
        return jnp.repeat(jnp.exp(draws), shape[position] // shards_of).reshape((-1,) + (1,) * (len(shape) - position - 1))

    level = one(*cuts[0])
    for cut in cuts[1:]:
        level = level * one(*cut)
    return level


def noise(key, extent, spread, limit, cuts=(), kind=jnp.bfloat16):
    factor_of = block_scale(key, extent, cuts, -0.22, 0.18) if cuts else 1.0
    array = jax.random.normal(key, extent, jnp.float32) * spread * factor_of
    return jnp.minimum(jnp.maximum(array, -limit), limit).astype(kind)


def setup_inputs(seed: int = 0) -> dict:
    seeds = jax.random.split(jax.random.key(seed), 6)
    small_w = noise(seeds[0], (SMALL, SMALL), SMALL ** -0.5, 0.09375, ((0, 16), (1, 8)))
    grow_a = noise(seeds[1], (BIG, SMALL), SMALL ** -0.5, 0.09375, ((0, 8), (1, 16)))
    grow_b = noise(seeds[2], (BIG, SMALL), SMALL ** -0.5, 0.09375, ((0, 16), (1, 8)))
    inputs = noise(seeds[3], (TOKENS, BIG), 1.0, 6.0, ((0, 2), (1, 16)))
    cotangent = noise(seeds[4], (TOKENS, BIG), (TOKENS ** -0.5), 0.1875, ((0, 2), (1, 8)))
    return {"small_w": small_w, "grow_a": grow_a, "grow_b": grow_b, "inputs": inputs, "cotangent": cotangent}


def summed(first_op, second_op, pieces):
    block_size = first_op.shape[1] // pieces

    def accumulate(running, block_index):
        begin_at = (block_index * block_size).astype(jnp.int32)
        left_block = lax.dynamic_slice_in_dim(first_op, begin_at, block_size, 1)
        right_block = lax.dynamic_slice_in_dim(second_op, begin_at, block_size, 0)
        product = jnp.dot(left_block, right_block, preferred_element_type=jnp.float32)
        rounded = lax.optimization_barrier(product.astype(jnp.bfloat16))
        return running + rounded.astype(jnp.float32), None

    initial = jnp.zeros((first_op.shape[0], second_op.shape[1]), jnp.float32)
    running, _ = lax.scan(accumulate, initial, jnp.arange(pieces, dtype=jnp.int32))
    return running


def reference(small_w, grow_a, grow_b, inputs, cotangent):
    projected = summed(grow_a, small_w, N_COL).astype(jnp.bfloat16)
    mapped = summed(grow_b, small_w.T, N_ROW).astype(jnp.bfloat16)
    big_weight = summed(projected, grow_b.T, N_DP).astype(jnp.bfloat16)
    grad_weight = summed(cotangent.T, inputs, N_DP).astype(jnp.bfloat16)
    outputs = summed(inputs, big_weight.T, N_COL).astype(jnp.bfloat16)
    grad_a = summed(grad_weight, mapped, N_COL)
    grad_b = summed(grad_weight.T, projected, N_ROW)
    return outputs, big_weight, grad_weight, grad_a, grad_b
```

```python
import jax
import jax.numpy as jnp
from jax import lax
from jax.sharding import PartitionSpec as P

BF = jnp.bfloat16
F32 = jnp.float32


def dot(a, b, da, db):
    return lax.dot_general(
        a, b, (((da,), (db,)), ((), ())), preferred_element_type=F32
    )


def rows(x, start, size):
    return lax.dynamic_slice_in_dim(x, start, size, 0)


def total(*terms):
    acc = terms[0].astype(F32)
    for term in terms[1:]:
        acc = acc + term.astype(F32)
    return acc


def body(small_w, grow_a, grow_b, inputs, cotangent):
    n_dp, n_row, n_col = (lax.axis_size(a) for a in ("dp", "row", "col"))
    d, r, c = (lax.axis_index(a) for a in ("dp", "row", "col"))
    n_y, n_z = n_row // 2, n_col // 2
    x_hi, y, core_id, z = r % 2, r // 2, c % 2, c // 2
    half = d ^ x_hi

    def permute(x, axis, size, target):
        return lax.ppermute(x, axis, [(i, target(i)) for i in range(size)])

    def core(x):
        return permute(x, "col", n_col, lambda i: i ^ 1)

    def z_flip(x, bit):
        return permute(x, "col", n_col, lambda i: i ^ (2 * bit))

    def from_z(x, k):
        return permute(x, "col", n_col, lambda i: (i - 2 * k) % n_col)

    def from_y(x, k):
        return permute(x, "row", n_row, lambda i: (i - 2 * k) % n_row)

    def x_pair(x):
        return permute(x, ("dp", "row"), n_dp * n_row, lambda i: (i ^ n_row) ^ 1)

    def x_far(x):
        return permute(x, "row", n_row, lambda i: i ^ 1)

    def other_dp(x):
        return permute(x, "dp", n_dp, lambda i: i ^ 1)

    def scatter_step(x, send, bit):
        n = x.shape[0] // 2
        mine = rows(x, bit * n, n)
        theirs = rows(x, (1 - bit) * n, n)
        return total(mine, send(theirs)).astype(BF)

    def gather_step(x, send, bit):
        theirs = send(x)
        low = jnp.where(bit == 0, x, theirs)
        high = jnp.where(bit == 0, theirs, x)
        return jnp.concatenate([low, high], 0)

    z_bits = [(lambda v, b=b: z_flip(v, b), (z // b) % 2) for b in (1, 2, 4)]
    col_steps = [(core, core_id)] + z_bits

    def col_scatter(x):
        for send, bit in col_steps:
            x = scatter_step(x, send, bit)
        return x

    def col_gather(x):
        for send, bit in reversed(col_steps):
            x = gather_step(x, send, bit)
        return x

    def row_sum(x):
        x = total(x, *[from_y(x, k) for k in range(1, n_y)]).astype(BF)
        return total(x, x_far(x)).astype(BF)

    w_half = rows(small_w, half * (small_w.shape[0] // 2), small_w.shape[0] // 2)
    w_own = jnp.concatenate([w_half] + [from_z(w_half, k) for k in range(1, n_z)], 0)
    w_all = jnp.concatenate([w_own, core(w_own)], 0)

    x_other = x_pair(inputs)
    c_other = other_dp(cotangent)

    u_part = dot(inputs, grow_b, 1, 0).astype(BF)
    q_part = dot(cotangent, grow_a, 1, 0).astype(BF)
    u = col_gather(col_scatter(u_part))
    q = row_sum(q_part)
    v = row_sum(dot(u, small_w, 1, 1).astype(BF))
    r_piece = col_scatter(dot(q, small_w, 1, 0).astype(BF))

    n_first = grow_b.shape[0] // 2
    ny = n_first // n_y
    nx = n_first // 2
    b_first = jnp.concatenate(
        [rows(grow_b, ((y + k) % n_y) * ny, ny) for k in range(n_y)], 0
    )
    part = dot(b_first, w_all, 1, 1).astype(BF)
    kept = total(
        part[:ny], *[from_y(part[k * ny : (k + 1) * ny], -k) for k in range(1, n_y)]
    )
    kept = scatter_step(kept.astype(BF), x_pair, x_hi)
    b_second = jnp.concatenate(
        [rows(grow_b, n_first + x_hi * nx, nx), rows(grow_b, n_first + (1 - x_hi) * nx, nx)], 0
    )
    part = dot(b_second, w_all, 1, 1).astype(BF)
    held = total(part[:nx], x_pair(part[nx:])).astype(BF)
    nxy = nx // n_y
    held = total(
        rows(held, y * nxy, nxy),
        *[from_y(rows(held, ((y + k) % n_y) * nxy, nxy), -k) for k in range(1, n_y)],
    ).astype(BF)

    def y_gather(x):
        n = x.shape[0]
        out = jnp.zeros((n * n_y, x.shape[1]), x.dtype)
        for k in range(n_y):
            piece = from_y(x, k) if k else x
            out = lax.dynamic_update_slice_in_dim(out, piece, ((y + k) % n_y) * n, 0)
        return out

    m_first = y_gather(gather_step(kept, x_pair, x_hi))
    m_second = gather_step(y_gather(held), x_pair, x_hi)
    m_all = jnp.concatenate([m_first, m_second], 0)

    n = grow_a.shape[1] // 2
    a_half = jnp.where(half == 0, grow_a[:, :n], grow_a[:, n:])
    a_own = jnp.concatenate([a_half] + [from_z(a_half, k) for k in range(1, n_z)], 1)
    a_other = core(a_own)
    depth = a_own.shape[1]

    def weight_rows(begin, size):
        own = dot(a_own[begin : begin + size], m_all[:, :depth], 1, 1)
        other = dot(a_other[begin : begin + size], m_all[:, depth:], 1, 1)
        piece = (own + other).astype(BF)
        return total(piece, other_dp(piece)).astype(BF)

    step = grow_a.shape[0] // 2
    big_weight = jnp.concatenate([weight_rows(i * step, step) for i in range(2)], 0)

    own = dot(cotangent, inputs, 0, 0).astype(BF)
    other = dot(c_other, x_other, 0, 0).astype(BF)
    grad_weight = total(own, other).astype(BF)

    dealt = v.reshape((2, 2, 2, 2, -1, v.shape[1])).transpose((3, 2, 1, 0, 4, 5))
    outputs = col_scatter(dot(dealt.reshape(v.shape), grow_a, 1, 1).astype(BF))

    def move(x, axis, size, parity):
        def target(i):
            a, b = divmod(i, size)
            return 2 * b + (a ^ parity)

        return permute(x, axis, n_dp * size, target)

    def relocate(x, axis, size):
        n = x.shape[1] // 2
        low, high = x[:, :n], x[:, n:]
        same = move(jnp.where(d == 0, low, high), axis, size, 0)
        swap = move(jnp.where(d == 0, high, low), axis, size, 1)
        bit = lax.axis_index(axis[1]) % 2
        first = jnp.where(bit == 0, same, swap)
        second = jnp.where(bit == 0, swap, same)
        return first, second

    v0, v1 = relocate(v, ("dp", "col"), n_col)
    v_own, v_other = jnp.where(d == 0, v0, v1), jnp.where(d == 0, v1, v0)
    grad_a = dot(cotangent, v_own, 0, 0) + dot(c_other, v_other, 0, 0)

    r0, r1 = relocate(r_piece, ("dp", "row"), n_row)
    r_own, r_other = jnp.where(d == 0, r0, r1), jnp.where(d == 0, r1, r0)
    r_both = col_gather(jnp.concatenate([r_own, r_other], 1))
    k = r_own.shape[1]
    grad_b = dot(inputs, r_both[:, :k], 0, 0) + dot(x_other, r_both[:, k:], 0, 0)
    return outputs, big_weight, grad_weight, grad_a, grad_b


def solution(mesh):
    return jax.shard_map(
        body,
        mesh=mesh,
        in_specs=(
            P("col", "row"),
            P("row", "col"),
            P("col", "row"),
            P("dp", "col"),
            P("dp", "row"),
        ),
        out_specs=(
            P(("dp", "col"), "row"),
            P("row", "col"),
            P("row", "col"),
            P("row", ("dp", "col")),
            P("col", ("dp", "row")),
        ),
        check_vma=False,
    )
```

```python
import jax
import jax.numpy as jnp
from jax import lax
from jax.sharding import PartitionSpec as P

BF = jnp.bfloat16
F32 = jnp.float32


def dot(a, b, da, db):
    return lax.dot_general(
        a, b, (((da,), (db,)), ((), ())), preferred_element_type=F32
    )


def rows(x, start, size):
    return lax.dynamic_slice_in_dim(x, start, size, 0)


def total(a, b):
    return (a.astype(F32) + b.astype(F32)).astype(BF)


def body(small_w, grow_a, grow_b, inputs, cotangent):
    n_dp, n_row, n_col = (lax.axis_size(a) for a in ("dp", "row", "col"))
    d, c = lax.axis_index("dp"), lax.axis_index("col")
    core_id = c % 2
    n_z = n_col // 2
    z_rings = [[2 * z + i for z in range(n_z)] for i in range(2)]

    def permute(x, axis, size, target):
        return lax.ppermute(x, axis, [(i, target(i)) for i in range(size)])

    def core(x):
        return permute(x, "col", n_col, lambda i: i ^ 1)

    def other_dp(x):
        return permute(x, "dp", n_dp, lambda i: i ^ 1)

    def exchange(x, axis):
        return lax.all_to_all(x, axis, 0, 0, tiled=True)

    def z_gather(x):
        return lax.all_gather(x, "col", axis=0, tiled=True, axis_index_groups=z_rings)

    def by_dp(own, other, axis):
        first = jnp.where(d == 0, own, other)
        second = jnp.where(d == 0, other, own)
        return jnp.stack([first, second], axis)

    n_w = small_w.shape[0] // 2
    w_own = z_gather(rows(small_w, d * n_w, n_w))
    w_other = core(w_own)

    tok = inputs.shape[0] // n_col
    x_other, c_other = other_dp(inputs), other_dp(cotangent)
    x_all = by_dp(
        inputs.reshape(n_col, tok, -1), x_other.reshape(n_col, tok, -1), 1
    ).reshape(n_dp * n_col * tok, -1)
    c_all = by_dp(
        cotangent.reshape(n_col, tok, -1), c_other.reshape(n_col, tok, -1), 1
    ).reshape(n_dp * n_col * tok, -1)

    u_part = dot(inputs, grow_b, 1, 0).astype(BF)
    q_part = dot(cotangent, grow_a, 1, 0).astype(BF)
    n_u = u_part.shape[1]
    got = exchange(jnp.concatenate([u_part, q_part], 1), "col").reshape(n_col, tok, -1)
    u_mine = got[:, :, :n_u].astype(F32).sum(0).astype(BF)
    q_got = got[:, :, n_u:]
    q_low, q_high = q_got[:, :, :n_w], q_got[:, :, n_w:]
    q_keep = jnp.where(d == 0, q_low, q_high)
    q_send = jnp.where(d == 0, q_high, q_low)
    u = by_dp(u_mine, other_dp(u_mine), 0).reshape(n_dp * tok, n_u)
    q = by_dp(q_keep, other_dp(q_send), 0)
    q = q.reshape(n_dp, n_z, 2, tok, n_w)
    q = jnp.where(core_id == 0, q, q[:, :, ::-1])
    q = q.transpose(0, 3, 2, 1, 4).reshape(n_dp * tok, n_col * n_w)

    w_all = jnp.concatenate([w_own, w_other], 0)
    width = w_all.shape[0]
    n_m = grow_b.shape[0] // n_row
    n_t = n_dp * tok // n_row
    left = jnp.concatenate(
        [grow_b.reshape(n_row, n_m, -1), u.reshape(n_row, n_t, -1)], 1
    ).reshape(n_row * (n_m + n_t), -1)
    part = dot(left, w_all, 1, 1).astype(BF).reshape(n_row, n_m + n_t, width)
    part = jnp.concatenate([part, q.reshape(n_row, n_t, width)], 1)
    got = exchange(part.reshape(-1, width), "row").reshape(n_row, -1, width)
    got = got.astype(F32).sum(0).astype(BF)

    m_all = lax.all_gather(got[:n_m], "row", axis=0, tiled=True)
    vq = jnp.broadcast_to(got[n_m:], (n_dp * n_row, 2 * n_t, width))
    vq = exchange(vq.reshape(-1, width), ("dp", "row"))
    vq = vq.reshape(n_dp, n_row, 2, n_t, width)
    v_both = vq[:, :, 0].reshape(n_dp, n_dp * tok, width)
    q_both = vq[:, :, 1].reshape(n_dp, n_dp * tok, width)
    v = lax.dynamic_index_in_dim(v_both, d, 0, keepdims=False)
    q = lax.dynamic_index_in_dim(q_both, d, 0, keepdims=False)

    r_part = dot(q, w_all, 1, 0).astype(BF)
    n_k = r_part.shape[1] // 2

    def move(x, parity):
        def target(i):
            a, b = divmod(i, n_row)
            return 2 * b + (a ^ parity)

        return permute(x, ("dp", "row"), n_dp * n_row, target)

    low, high = r_part[:, :n_k], r_part[:, n_k:]
    r_piece = total(
        move(jnp.where(d == 0, low, high), 0), move(jnp.where(d == 0, high, low), 1)
    )

    v_cols = v_both.reshape(n_dp, n_dp * tok, 2, n_z, n_w)
    v_cols = jnp.where(core_id == 0, v_cols, v_cols[:, :, ::-1])
    v_cols = lax.dynamic_slice_in_dim(v_cols, d * (n_z // 2), n_z // 2, 3)
    v_cols = v_cols.transpose(3, 2, 0, 1, 4).reshape(n_col, n_dp * tok, n_w)
    r_rep = jnp.broadcast_to(r_piece, (n_col,) + r_piece.shape)
    sent = jnp.concatenate([r_rep, v_cols], 2).reshape(-1, n_k + n_w)
    got = exchange(sent, "col")
    grad_b = dot(x_all, got[:, :n_k], 0, 0)
    grad_a = dot(c_all, got[:, n_k:], 0, 0)

    a_half = jnp.where(d == 0, grow_a[:, :n_w], grow_a[:, n_w:]).T
    a_half, _ = lax.optimization_barrier((a_half, w_own))
    a_own = z_gather(a_half)
    a_all = jnp.concatenate([a_own, core(a_own)], 0)

    y_part = dot(v, a_all, 1, 0).astype(BF)
    outputs = total(
        rows(y_part, d * tok, tok), other_dp(rows(y_part, (1 - d) * tok, tok))
    )

    def weight_rows(i, n):
        piece = dot(a_all[:, i * n : (i + 1) * n], m_all, 0, 1).astype(BF)
        return total(piece, other_dp(piece))

    n = grow_a.shape[0] // 2
    big_weight = jnp.concatenate([weight_rows(i, n) for i in range(2)], 0)
    grad_weight = dot(c_all, x_all, 0, 0).astype(BF)
    return outputs, big_weight, grad_weight, grad_a, grad_b


def solution(mesh):
    return jax.shard_map(
        body,
        mesh=mesh,
        in_specs=(
            P("col", "row"),
            P("row", "col"),
            P("col", "row"),
            P("dp", "col"),
            P("dp", "row"),
        ),
        out_specs=(
            P(("dp", "col"), "row"),
            P("row", "col"),
            P("row", "col"),
            P("row", ("dp", "col")),
            P("col", ("dp", "row")),
        ),
        check_vma=False,
    )
```

```python
import jax
import jax.numpy as jnp
from jax import lax
from jax.sharding import PartitionSpec as P

BF = jnp.bfloat16
F32 = jnp.float32


def dot(a, b, da, db):
    return lax.dot_general(
        a, b, (((da,), (db,)), ((), ())), preferred_element_type=F32
    )


def rows(x, start, size):
    return lax.dynamic_slice_in_dim(x, start, size, 0)


def total(a, b):
    return (a.astype(F32) + b.astype(F32)).astype(BF)


def body(small_w, grow_a, grow_b, inputs, cotangent):
    n_dp, n_row, n_col = (lax.axis_size(a) for a in ("dp", "row", "col"))
    d, c = lax.axis_index("dp"), lax.axis_index("col")
    core_id = c % 2
    n_z = n_col // 2
    z_rings = [[2 * z + i for z in range(n_z)] for i in range(2)]

    def permute(x, axis, size, target):
        return lax.ppermute(x, axis, [(i, target(i)) for i in range(size)])

    def core(x):
        return permute(x, "col", n_col, lambda i: i ^ 1)

    def other_dp(x):
        return permute(x, "dp", n_dp, lambda i: i ^ 1)

    def from_y(x, k):
        return permute(x, "row", n_row, lambda i: (i - 2 * k) % n_row)

    def x_far(x):
        return permute(x, "row", n_row, lambda i: i ^ 1)

    def from_z(x, k):
        return permute(x, "col", n_col, lambda i: (i - 2 * k) % n_col) if k else x

    def exchange(x, axis, groups=None):
        return lax.all_to_all(x, axis, 0, 0, tiled=True, axis_index_groups=groups)

    def scatter_sum(x, axis, size):
        got = exchange(x, axis).reshape(size, -1, x.shape[1])
        return got.astype(F32).sum(0).astype(BF)

    def gather(x, axis, size):
        return exchange(jnp.broadcast_to(x, (size,) + x.shape).reshape(-1, x.shape[1]), axis)

    def assemble(pieces, first):
        n = pieces[0].shape[0]
        out = jnp.zeros((n * len(pieces), pieces[0].shape[1]), BF)
        for k, piece in enumerate(pieces):
            at = (first + k) % len(pieces) * n
            out = lax.dynamic_update_slice_in_dim(out, piece, at, 0)
        return out

    def z_assemble(x):
        return assemble([from_z(x, k) for k in range(n_z)], c // 2)

    def z_gather(x):
        return lax.all_gather(x, "col", axis=0, tiled=True, axis_index_groups=z_rings)

    def both_cores(own):
        other = core(own)
        low = jnp.where(core_id == 0, own, other)
        high = jnp.where(core_id == 0, other, own)
        return jnp.concatenate([low, high], 0)

    def x_pair(x):
        return permute(x, ("dp", "row"), n_dp * n_row, lambda i: (i ^ n_row) ^ 1)

    def by_dp(own, other):
        n = own.shape[0] // n_col
        own = own.reshape(n_col, n, -1)
        other = other.reshape(n_col, n, -1)
        first = jnp.where(d == 0, own, other)
        second = jnp.where(d == 0, other, own)
        return jnp.stack([first, second], 1).reshape(n_dp * n_col * n, -1)

    n_w = small_w.shape[0] // 2
    w_half = rows(small_w, d * n_w, n_w)
    w_own = z_gather(w_half)
    q_mine = scatter_sum(dot(cotangent, grow_a, 1, 0).astype(BF), "row", n_row)
    q = gather(q_mine, "row", n_row)
    x_other, c_other = x_pair(inputs), other_dp(cotangent)
    w_own, q, x_other, c_other = lax.optimization_barrier(
        (w_own, q, x_other, c_other)
    )
    w_all = both_cores(w_own)

    tok = inputs.shape[0] // n_col
    x_all = by_dp(inputs, x_other)

    part = dot(w_all, grow_b, 1, 1).astype(BF)
    n_m, n_n = part.shape[0] // n_row, part.shape[1]
    a_half = jnp.where(d == 0, grow_a[:, :n_w], grow_a[:, n_w:]).T
    a_half, _ = lax.optimization_barrier((a_half, w_own))
    a_own = z_gather(a_half)
    m_slice = scatter_sum(part, "row", n_row)
    x_hi = lax.axis_index("row") % 2
    m_other = x_far(m_slice)
    m_pair = jnp.concatenate(
        [jnp.where(x_hi == 0, m_slice, m_other), jnp.where(x_hi == 0, m_other, m_slice)], 0
    )
    m_pieces = [m_pair] + [from_y(m_pair, k) for k in range(1, n_row // 2)]
    m_all = assemble(m_pieces, lax.axis_index("row") // 2)

    r_part = dot(q, small_w, 1, 0).astype(BF)
    n_k = r_part.shape[1] // 2
    v_part = dot(x_all, m_slice, 1, 1).astype(BF)
    n_s = v_part.shape[1]
    both = jnp.concatenate(
        [
            r_part[:, :n_k].reshape(n_z, 2, tok, n_k),
            r_part[:, n_k:].reshape(n_z, 2, tok, n_k),
            v_part.reshape(n_z, 2, n_dp * tok, n_s),
        ],
        2,
    )
    keep = jnp.where(core_id == 0, both[:, 0], both[:, 1])
    send = jnp.where(core_id == 0, both[:, 1], both[:, 0])
    both = total(keep, core(send)).reshape(-1, n_s)
    both = exchange(both, "col", z_rings).reshape(n_z, -1, n_s)
    both = both.astype(F32).sum(0).astype(BF)
    low, high, v_mine = both[:tok], both[tok : 2 * tok], both[2 * tok :]

    def move(x, parity):
        def target(i):
            a, b = divmod(i, n_row)
            return 2 * b + (a ^ parity)

        return permute(x, ("dp", "row"), n_dp * n_row, target)

    same = move(jnp.where(d == 0, low, high), 0)
    swap = move(jnp.where(d == 0, high, low), 1)
    r_piece = jnp.concatenate(
        [jnp.where(x_hi == 0, same, swap), jnp.where(x_hi == 0, swap, same)], 0
    )
    v_both = gather(v_mine, ("dp", "row"), n_dp * n_row)
    v_both, m_all, a_own = lax.optimization_barrier((v_both, m_all, a_own))
    c_all = by_dp(cotangent, c_other)
    v_both = v_both.reshape(n_dp, n_row, n_dp * tok, n_s)
    v = lax.dynamic_index_in_dim(v_both, d, 0, keepdims=False)
    v = v.transpose(1, 0, 2).reshape(n_dp * tok, n_row * n_s)

    v_cols = v_both.reshape(n_dp, 2, n_z // 2, n_dp * tok, 2, n_w)
    v_cols = lax.dynamic_slice_in_dim(v_cols, d * (n_z // 4), n_z // 4, 2)
    v_cols = v_cols.transpose(2, 4, 1, 0, 3, 5).reshape(n_col, n_dp * tok, n_w)
    r_rep = jnp.broadcast_to(r_piece, (n_col,) + r_piece.shape)
    sent = jnp.concatenate([r_rep, v_cols], 2).reshape(-1, n_k + n_w)
    got = exchange(sent, "col")
    a_all = both_cores(a_own)
    n = grow_a.shape[0] // 2
    parts = [
        dot(a_all[:, i * n : (i + 1) * n], m_all, 0, 0).astype(BF) for i in range(2)
    ]
    big_weight = jnp.concatenate([total(p, other_dp(p)) for p in parts], 0)
    got, big_weight = lax.optimization_barrier((got, big_weight))
    grad_b = dot(x_all, got[:, :n_k], 0, 0)
    grad_a = dot(c_all, got[:, n_k:], 0, 0)

    y_part = dot(v, a_all, 1, 0).astype(BF)
    outputs = total(
        rows(y_part, d * tok, tok), other_dp(rows(y_part, (1 - d) * tok, tok))
    )

    grad_weight = dot(c_all, x_all, 0, 0).astype(BF)
    return outputs, big_weight, grad_weight, grad_a, grad_b


def solution(mesh):
    return jax.shard_map(
        body,
        mesh=mesh,
        in_specs=(
            P("col", "row"),
            P("row", "col"),
            P("col", "row"),
            P("dp", "col"),
            P("dp", "row"),
        ),
        out_specs=(
            P(("dp", "col"), "row"),
            P("row", "col"),
            P("row", "col"),
            P("row", ("dp", "col")),
            P("col", ("dp", "row")),
        ),
        check_vma=False,
    )
```

```python
import jax
import jax.numpy as jnp
from jax import lax
from jax.sharding import PartitionSpec as P

BF = jnp.bfloat16
F32 = jnp.float32


def dot(a, b, da, db):
    return lax.dot_general(
        a, b, (((da,), (db,)), ((), ())), preferred_element_type=F32
    )


def rows(x, start, size):
    return lax.dynamic_slice_in_dim(x, start, size, 0)


def total(a, b):
    return (a.astype(F32) + b.astype(F32)).astype(BF)


def body(small_w, grow_a, grow_b, inputs, cotangent):
    n_dp, n_row, n_col = (lax.axis_size(a) for a in ("dp", "row", "col"))
    d, c = lax.axis_index("dp"), lax.axis_index("col")
    core_id = c % 2
    n_z = n_col // 2
    z_rings = [[2 * z + i for z in range(n_z)] for i in range(2)]

    def permute(x, axis, size, target):
        return lax.ppermute(x, axis, [(i, target(i)) for i in range(size)])

    def core(x):
        return permute(x, "col", n_col, lambda i: i ^ 1)

    def other_dp(x):
        return permute(x, "dp", n_dp, lambda i: i ^ 1)

    def from_y(x, k):
        return permute(x, "row", n_row, lambda i: (i - 2 * k) % n_row)

    def x_far(x):
        return permute(x, "row", n_row, lambda i: i ^ 1)

    def from_z(x, k):
        return permute(x, "col", n_col, lambda i: (i - 2 * k) % n_col) if k else x

    def exchange(x, axis, groups=None):
        return lax.all_to_all(x, axis, 0, 0, tiled=True, axis_index_groups=groups)

    def scatter_sum(x, axis, size):
        got = exchange(x, axis).reshape(size, -1, x.shape[1])
        return got.astype(F32).sum(0).astype(BF)

    def gather(x, axis, size, groups=None):
        copies = jnp.broadcast_to(x, (size,) + x.shape).reshape(-1, x.shape[1])
        return exchange(copies, axis, groups)

    def assemble(pieces, first):
        n = pieces[0].shape[0]
        out = jnp.zeros((n * len(pieces), pieces[0].shape[1]), BF)
        for k, piece in enumerate(pieces):
            at = (first + k) % len(pieces) * n
            out = lax.dynamic_update_slice_in_dim(out, piece, at, 0)
        return out

    def z_assemble(x):
        return assemble([from_z(x, k) for k in range(n_z)], c // 2)

    def z_gather(x):
        return lax.all_gather(x, "col", axis=0, tiled=True, axis_index_groups=z_rings)

    def by_core(own, other):
        low = jnp.where(core_id == 0, own, other)
        high = jnp.where(core_id == 0, other, own)
        return jnp.concatenate([low, high], 0)

    def x_pair(x):
        return permute(x, ("dp", "row"), n_dp * n_row, lambda i: (i ^ n_row) ^ 1)

    def by_dp(own, other):
        n = own.shape[0] // n_col
        own = own.reshape(n_col, n, -1)
        other = other.reshape(n_col, n, -1)
        first = jnp.where(d == 0, own, other)
        second = jnp.where(d == 0, other, own)
        return jnp.stack([first, second], 1).reshape(n_dp * n_col * n, -1)

    n_w = small_w.shape[0] // 2
    w_half = rows(small_w, d * n_w, n_w)
    w_own = gather(w_half, "col", n_z, z_rings)
    q_part = dot(cotangent, grow_a, 1, 0).astype(BF)
    q = q_part.astype(F32)
    for k in range(1, n_row // 2):
        q = q + from_y(q_part, k).astype(F32)
    q = q.astype(BF)
    q = total(q, x_far(q))
    n_c = cotangent.shape[0] // 2
    c_piece = other_dp(rows(cotangent, core_id * n_c, n_c))
    w_own, q, x_other, c_piece = lax.optimization_barrier(
        (w_own, q, x_pair(inputs), c_piece)
    )
    w_all = by_core(w_own, core(w_own))

    tok = inputs.shape[0] // n_col
    x_all = by_dp(inputs, x_other)

    part = dot(w_all, grow_b, 1, 1).astype(BF)
    n_m, n_n = part.shape[0] // n_row, part.shape[1]
    a_half = jnp.where(d == 0, grow_a[:, :n_w], grow_a[:, n_w:]).T
    a_half, _ = lax.optimization_barrier((a_half, w_own))
    a_own = z_gather(a_half)
    m_slice = scatter_sum(part, "row", n_row)
    c_all = by_dp(cotangent, by_core(c_piece, core(c_piece)))
    m_slice, c_all = lax.optimization_barrier((m_slice, c_all))
    grad_weight = dot(c_all, x_all, 0, 0).astype(BF)
    x_hi = lax.axis_index("row") % 2
    m_other = x_far(m_slice)
    m_pair = jnp.concatenate(
        [jnp.where(x_hi == 0, m_slice, m_other), jnp.where(x_hi == 0, m_other, m_slice)], 0
    )
    m_pieces = [m_pair] + [from_y(m_pair, k) for k in range(1, n_row // 2)]

    r_part = dot(q, small_w, 1, 0).astype(BF)
    n_k = r_part.shape[1] // 2
    v_part = dot(x_all, m_slice, 1, 1).astype(BF)
    n_s = v_part.shape[1]
    both = jnp.concatenate(
        [
            r_part[:, :n_k].reshape(n_z, 2, tok, n_k),
            r_part[:, n_k:].reshape(n_z, 2, tok, n_k),
            v_part.reshape(n_z, 2, n_dp * tok, n_s),
        ],
        2,
    )
    keep = jnp.where(core_id == 0, both[:, 0], both[:, 1])
    send = jnp.where(core_id == 0, both[:, 1], both[:, 0])
    both = total(keep, core(send)).reshape(-1, n_s)
    both = exchange(both, "col", z_rings).reshape(n_z, -1, n_s)
    both, a_own, grad_weight, *m_pieces = lax.optimization_barrier(
        (both, a_own, grad_weight, *m_pieces)
    )
    n_y = n_row // 2
    m_all = assemble(m_pieces, lax.axis_index("row") // 2 + core_id * (n_y // 2))
    both = both.astype(F32).sum(0).astype(BF)
    low, high, v_mine = both[:tok], both[tok : 2 * tok], both[2 * tok :]

    places = n_dp * n_row
    r_low_high = jnp.stack([low, high])
    sent = jnp.concatenate(
        [
            jnp.broadcast_to(v_mine, (places,) + v_mine.shape),
            jnp.broadcast_to(r_low_high, (places // 2,) + r_low_high.shape).reshape(
                places, tok, n_k
            ),
        ],
        1,
    )
    got = exchange(sent.reshape(-1, n_s), ("dp", "row"))
    a_other = core(a_own)
    depth = a_own.shape[0]
    parts = []
    for cut in (slice(0, a_own.shape[1] // 4), slice(a_own.shape[1] // 4, None)):
        part = dot(a_own[:, cut], m_all[:depth], 0, 0)
        part = part + dot(a_other[:, cut], m_all[depth:], 0, 0)
        parts.append(part.astype(BF))
    got, first, *parts = lax.optimization_barrier((got, other_dp(parts[0]), *parts))
    got = got.reshape(n_dp, n_row, (n_dp + 1) * tok, n_s)
    v_both = got[:, :, : n_dp * tok]
    source = d * (n_row // 2) + lax.axis_index("row") // 2
    r_piece = lax.dynamic_slice(got, (0, source, n_dp * tok, 0), (n_dp, 1, tok, n_k))
    r_piece = r_piece.reshape(n_dp * tok, n_k)
    v = lax.dynamic_index_in_dim(v_both, d, 0, keepdims=False)
    v = v.transpose(1, 0, 2).reshape(n_dp * tok, n_row * n_s)

    v_cols = v_both.reshape(n_dp, 2, n_z // 2, n_dp * tok, 2, n_w)
    v_cols = lax.dynamic_slice_in_dim(v_cols, d * (n_z // 4), n_z // 4, 2)
    v_cols = v_cols.transpose(2, 4, 1, 0, 3, 5).reshape(n_col, n_dp * tok, n_w)
    r_rep = jnp.broadcast_to(r_piece, (n_col,) + r_piece.shape)
    sent = jnp.concatenate([r_rep, v_cols], 2).reshape(-1, n_k + n_w)
    got = exchange(sent, "col")
    second = other_dp(parts[1])
    big_weight = jnp.concatenate([total(parts[0], first), total(parts[1], second)], 0)
    got, big_weight = lax.optimization_barrier((got, big_weight))
    grad_b = dot(x_all, got[:, :n_k], 0, 0)
    grad_a = dot(c_all, got[:, n_k:], 0, 0)

    low, high = v[:, :depth], v[:, depth:]
    v_own = jnp.where(core_id == 0, low, high)
    v_rest = jnp.where(core_id == 0, high, low)
    y_part = (dot(v_own, a_own, 1, 0) + dot(v_rest, a_other, 1, 0)).astype(BF)
    outputs = total(
        rows(y_part, d * tok, tok), other_dp(rows(y_part, (1 - d) * tok, tok))
    )

    return outputs, big_weight, grad_weight, grad_a, grad_b


def solution(mesh):
    return jax.shard_map(
        body,
        mesh=mesh,
        in_specs=(
            P("col", "row"),
            P("row", "col"),
            P("col", "row"),
            P("dp", "col"),
            P("dp", "row"),
        ),
        out_specs=(
            P(("dp", "col"), "row"),
            P("row", "col"),
            P("row", "col"),
            P("row", ("dp", "col")),
            P("col", ("dp", "row")),
        ),
        check_vma=False,
    )
```

```python
import jax
import jax.numpy as jnp
from jax import lax
from jax.sharding import PartitionSpec as P

BF = jnp.bfloat16
F32 = jnp.float32


def dot(a, b, da, db):
    return lax.dot_general(
        a, b, (((da,), (db,)), ((), ())), preferred_element_type=F32
    )


def rows(x, start, size):
    return lax.dynamic_slice_in_dim(x, start, size, 0)


def total(a, b):
    return (a.astype(F32) + b.astype(F32)).astype(BF)


def body(small_w, grow_a, grow_b, inputs, cotangent):
    n_dp, n_row, n_col = (lax.axis_size(a) for a in ("dp", "row", "col"))
    d, c = lax.axis_index("dp"), lax.axis_index("col")
    core_id = c % 2
    n_z = n_col // 2
    z_rings = [[2 * z + i for z in range(n_z)] for i in range(2)]

    def permute(x, axis, size, target):
        return lax.ppermute(x, axis, [(i, target(i)) for i in range(size)])

    def core(x):
        return permute(x, "col", n_col, lambda i: i ^ 1)

    def other_dp(x):
        return permute(x, "dp", n_dp, lambda i: i ^ 1)

    def from_y(x, k):
        return permute(x, "row", n_row, lambda i: (i - 2 * k) % n_row)

    def x_far(x):
        return permute(x, "row", n_row, lambda i: i ^ 1)

    def exchange(x, axis, groups=None):
        return lax.all_to_all(x, axis, 0, 0, tiled=True, axis_index_groups=groups)

    def scatter_sum(x, axis, size):
        got = exchange(x, axis).reshape(size, -1, x.shape[1])
        return got.astype(F32).sum(0).astype(BF)

    def gather(x, axis, size, groups=None):
        copies = jnp.broadcast_to(x, (size,) + x.shape).reshape(-1, x.shape[1])
        return exchange(copies, axis, groups)

    def assemble(pieces, first):
        n = pieces[0].shape[0]
        out = jnp.zeros((n * len(pieces), pieces[0].shape[1]), BF)
        for k, piece in enumerate(pieces):
            at = (first + k) % len(pieces) * n
            out = lax.dynamic_update_slice_in_dim(out, piece, at, 0)
        return out

    def z_gather(x):
        return lax.all_gather(x, "col", axis=0, tiled=True, axis_index_groups=z_rings)

    def by_core(own, other):
        low = jnp.where(core_id == 0, own, other)
        high = jnp.where(core_id == 0, other, own)
        return jnp.concatenate([low, high], 0)

    def x_pair(x):
        return permute(x, ("dp", "row"), n_dp * n_row, lambda i: (i ^ n_row) ^ 1)

    def by_dp(own, other):
        n = own.shape[0] // n_col
        own = own.reshape(n_col, n, -1)
        other = other.reshape(n_col, n, -1)
        first = jnp.where(d == 0, own, other)
        second = jnp.where(d == 0, other, own)
        return jnp.stack([first, second], 1).reshape(n_dp * n_col * n, -1)

    n_w = small_w.shape[0] // 2
    w_half = rows(small_w, d * n_w, n_w)
    w_own = gather(w_half, "col", n_z, z_rings)
    q_part = dot(cotangent, grow_a, 1, 0).astype(BF)
    q = q_part.astype(F32)
    for k in range(1, n_row // 2):
        q = q + from_y(q_part, k).astype(F32)
    q = q.astype(BF)
    q = total(q, x_far(q))
    n_c = cotangent.shape[0] // 2
    c_piece = other_dp(rows(cotangent, core_id * n_c, n_c))
    w_own, q, x_other, c_piece = lax.optimization_barrier(
        (w_own, q, x_pair(inputs), c_piece)
    )
    w_all = by_core(w_own, core(w_own))

    tok = inputs.shape[0] // n_col
    x_all = by_dp(inputs, x_other)

    part = dot(w_all, grow_b, 1, 1).astype(BF)
    n_m, n_n = part.shape[0] // n_row, part.shape[1]
    a_half = jnp.where(d == 0, grow_a[:, :n_w], grow_a[:, n_w:]).T
    a_half, _ = lax.optimization_barrier((a_half, w_own))
    a_own = z_gather(a_half)
    m_slice = scatter_sum(part, "row", n_row)
    c_all = by_dp(cotangent, by_core(c_piece, core(c_piece)))
    m_slice, c_all = lax.optimization_barrier((m_slice, c_all))
    grad_weight = dot(c_all, x_all, 0, 0).astype(BF)
    x_hi = lax.axis_index("row") % 2
    m_other = x_far(m_slice)
    m_pair = jnp.concatenate(
        [jnp.where(x_hi == 0, m_slice, m_other), jnp.where(x_hi == 0, m_other, m_slice)], 0
    )
    m_pieces = [m_pair] + [from_y(m_pair, k) for k in range(1, n_row // 2)]

    r_part = dot(q, small_w, 1, 0).astype(BF)
    n_k = r_part.shape[1] // 2
    v_part = dot(x_all, m_slice, 1, 1).astype(BF)
    n_s = v_part.shape[1]
    both = jnp.concatenate(
        [
            r_part[:, :n_k].reshape(n_z, 2, tok, n_k),
            r_part[:, n_k:].reshape(n_z, 2, tok, n_k),
            v_part.reshape(n_z, 2, n_dp * tok, n_s),
        ],
        2,
    )
    keep = jnp.where(core_id == 0, both[:, 0], both[:, 1])
    send = jnp.where(core_id == 0, both[:, 1], both[:, 0])
    both = total(keep, core(send)).reshape(-1, n_s)
    both = exchange(both, "col", z_rings).reshape(n_z, -1, n_s)
    both, a_own, grad_weight, *m_pieces = lax.optimization_barrier(
        (both, a_own, grad_weight, *m_pieces)
    )
    n_y = n_row // 2
    m_all = assemble(m_pieces, lax.axis_index("row") // 2 + core_id * (n_y // 2))
    both = both.astype(F32).sum(0).astype(BF)
    low, high, v_mine = both[:tok], both[tok : 2 * tok], both[2 * tok :]

    places = n_dp * n_row
    r_low_high = jnp.stack([low, high])
    sent = jnp.concatenate(
        [
            jnp.broadcast_to(v_mine, (places,) + v_mine.shape),
            jnp.broadcast_to(r_low_high, (places // 2,) + r_low_high.shape).reshape(
                places, tok, n_k
            ),
        ],
        1,
    )
    got = exchange(sent.reshape(-1, n_s), ("dp", "row"))
    a_other = core(a_own)
    depth = a_own.shape[0]
    parts = []
    for cut in (slice(0, a_own.shape[1] // 8), slice(a_own.shape[1] // 8, None)):
        part = dot(a_own[:, cut], m_all[:depth], 0, 0)
        part = part + dot(a_other[:, cut], m_all[depth:], 0, 0)
        parts.append(part.astype(BF))
    got, first, *parts = lax.optimization_barrier((got, other_dp(parts[0]), *parts))
    got = got.reshape(n_dp, n_row, (n_dp + 1) * tok, n_s)
    source = d * (n_row // 2) + lax.axis_index("row") // 2
    r_piece = lax.dynamic_slice(got, (0, source, n_dp * tok, 0), (n_dp, 1, tok, n_k))
    r_piece = r_piece.reshape(n_dp * tok, n_k)
    v = lax.dynamic_slice(got, (d, 0, 0, 0), (1, n_row, n_dp * tok, n_s))
    v = v[0].transpose(1, 0, 2).reshape(n_dp * tok, n_row * n_s)

    v_cols = got.reshape(n_dp, 2, n_z // 2, (n_dp + 1) * tok, 2, n_w)
    v_cols = lax.dynamic_slice(
        v_cols,
        (0, 0, d * (n_z // 4), 0, 0, 0),
        (n_dp, 2, n_z // 4, n_dp * tok, 2, n_w),
    )
    v_cols = v_cols.transpose(2, 4, 1, 0, 3, 5).reshape(n_col, n_dp * tok, n_w)
    r_rep = jnp.broadcast_to(r_piece, (n_col,) + r_piece.shape)
    sent = jnp.concatenate([r_rep, v_cols], 2).reshape(-1, n_k + n_w)
    got = exchange(sent, "col")
    second = other_dp(parts[1])
    big_weight = jnp.concatenate([total(parts[0], first), total(parts[1], second)], 0)
    got, big_weight = lax.optimization_barrier((got, big_weight))
    grad_b = dot(x_all, got[:, :n_k], 0, 0)
    grad_a = dot(c_all, got[:, n_k:], 0, 0)

    low, high = v[:, :depth], v[:, depth:]
    v_own = jnp.where(core_id == 0, low, high)
    v_rest = jnp.where(core_id == 0, high, low)
    y_part = (dot(v_own, a_own, 1, 0) + dot(v_rest, a_other, 1, 0)).astype(BF)
    outputs = total(
        rows(y_part, d * tok, tok), other_dp(rows(y_part, (1 - d) * tok, tok))
    )

    return outputs, big_weight, grad_weight, grad_a, grad_b


def solution(mesh):
    return jax.shard_map(
        body,
        mesh=mesh,
        in_specs=(
            P("col", "row"),
            P("row", "col"),
            P("col", "row"),
            P("dp", "col"),
            P("dp", "row"),
        ),
        out_specs=(
            P(("dp", "col"), "row"),
            P("row", "col"),
            P("row", "col"),
            P("row", ("dp", "col")),
            P("col", ("dp", "row")),
        ),
        check_vma=False,
    )
```

```python
import jax
import jax.numpy as jnp
from jax import lax
from jax.sharding import PartitionSpec as P

BF = jnp.bfloat16
F32 = jnp.float32


def dot(a, b, da, db):
    return lax.dot_general(
        a, b, (((da,), (db,)), ((), ())), preferred_element_type=F32
    )


def rows(x, start, size):
    return lax.dynamic_slice_in_dim(x, start, size, 0)


def total(a, b):
    return (a.astype(F32) + b.astype(F32)).astype(BF)


def body(small_w, grow_a, grow_b, inputs, cotangent):
    n_dp, n_row, n_col = (lax.axis_size(a) for a in ("dp", "row", "col"))
    d, c = lax.axis_index("dp"), lax.axis_index("col")
    core_id = c % 2
    n_z = n_col // 2
    z_rings = [[2 * z + i for z in range(n_z)] for i in range(2)]

    def permute(x, axis, size, target):
        return lax.ppermute(x, axis, [(i, target(i)) for i in range(size)])

    def core(x):
        return permute(x, "col", n_col, lambda i: i ^ 1)

    def other_dp(x):
        return permute(x, "dp", n_dp, lambda i: i ^ 1)

    def from_y(x, k):
        return permute(x, "row", n_row, lambda i: (i - 2 * k) % n_row)

    def x_far(x):
        return permute(x, "row", n_row, lambda i: i ^ 1)

    def exchange(x, axis, groups=None):
        return lax.all_to_all(x, axis, 0, 0, tiled=True, axis_index_groups=groups)

    def scatter_sum(x, axis, size):
        got = exchange(x, axis).reshape(size, -1, x.shape[1])
        return got.astype(F32).sum(0).astype(BF)

    def gather(x, axis, size, groups=None):
        copies = jnp.broadcast_to(x, (size,) + x.shape).reshape(-1, x.shape[1])
        return exchange(copies, axis, groups)

    def assemble(pieces, first):
        n = pieces[0].shape[0]
        out = jnp.zeros((n * len(pieces), pieces[0].shape[1]), BF)
        for k, piece in enumerate(pieces):
            at = (first + k) % len(pieces) * n
            out = lax.dynamic_update_slice_in_dim(out, piece, at, 0)
        return out

    def z_gather(x):
        return lax.all_gather(x, "col", axis=0, tiled=True, axis_index_groups=z_rings)

    def by_core(own, other):
        low = jnp.where(core_id == 0, own, other)
        high = jnp.where(core_id == 0, other, own)
        return jnp.concatenate([low, high], 0)

    def x_pair(x):
        return permute(x, ("dp", "row"), n_dp * n_row, lambda i: (i ^ n_row) ^ 1)

    def by_dp(own, other):
        n = own.shape[0] // n_col
        own = own.reshape(n_col, n, -1)
        other = other.reshape(n_col, n, -1)
        first = jnp.where(d == 0, own, other)
        second = jnp.where(d == 0, other, own)
        return jnp.stack([first, second], 1).reshape(n_dp * n_col * n, -1)

    n_w = small_w.shape[0] // 2
    w_half = rows(small_w, d * n_w, n_w)
    w_own = gather(w_half, "col", n_z, z_rings)
    q_part = dot(cotangent, grow_a, 1, 0).astype(BF)
    q = q_part.astype(F32)
    for k in range(1, n_row // 2):
        q = q + from_y(q_part, k).astype(F32)
    q = q.astype(BF)
    q = total(q, x_far(q))
    n_c = cotangent.shape[0] // 2
    c_piece = other_dp(rows(cotangent, core_id * n_c, n_c))
    w_own, q, x_other, c_piece = lax.optimization_barrier(
        (w_own, q, x_pair(inputs), c_piece)
    )
    w_all = by_core(w_own, core(w_own))

    tok = inputs.shape[0] // n_col
    x_all = by_dp(inputs, x_other)

    part = dot(w_all, grow_b, 1, 1).astype(BF)
    n_m, n_n = part.shape[0] // n_row, part.shape[1]
    a_half = jnp.where(d == 0, grow_a[:, :n_w], grow_a[:, n_w:]).T
    a_half, _ = lax.optimization_barrier((a_half, w_own))
    a_own = z_gather(a_half)
    m_slice = scatter_sum(part, "row", n_row)
    c_all = by_dp(cotangent, by_core(c_piece, core(c_piece)))
    m_slice, c_all = lax.optimization_barrier((m_slice, c_all))
    grad_weight = dot(c_all, x_all, 0, 0).astype(BF)
    x_hi = lax.axis_index("row") % 2
    m_other = x_far(m_slice)
    m_pair = jnp.concatenate(
        [jnp.where(x_hi == 0, m_slice, m_other), jnp.where(x_hi == 0, m_other, m_slice)], 0
    )
    m_pieces = [m_pair] + [from_y(m_pair, k) for k in range(1, n_row // 2)]

    r_part = dot(q, small_w, 1, 0).astype(BF)
    n_k = r_part.shape[1] // 2
    v_part = dot(x_all, m_slice, 1, 1).astype(BF)
    n_s = v_part.shape[1]
    both = jnp.concatenate(
        [
            r_part[:, :n_k].reshape(n_z, 2, tok, n_k),
            r_part[:, n_k:].reshape(n_z, 2, tok, n_k),
            v_part.reshape(n_z, 2, n_dp * tok, n_s),
        ],
        2,
    )
    keep = jnp.where(core_id == 0, both[:, 0], both[:, 1])
    send = jnp.where(core_id == 0, both[:, 1], both[:, 0])
    both = total(keep, core(send)).reshape(-1, n_s)
    both = exchange(both, "col", z_rings).reshape(n_z, -1, n_s)
    both, a_own, grad_weight, x_t, c_t, *m_pieces = lax.optimization_barrier(
        (both, a_own, grad_weight, x_all.T, c_all.T, *m_pieces)
    )
    n_y = n_row // 2
    m_all = assemble(m_pieces, lax.axis_index("row") // 2 + core_id * (n_y // 2))
    both = both.astype(F32).sum(0).astype(BF)
    low, high, v_mine = both[:tok], both[tok : 2 * tok], both[2 * tok :]

    places = n_dp * n_row
    r_low_high = jnp.stack([low, high])
    sent = jnp.concatenate(
        [
            jnp.broadcast_to(v_mine, (places,) + v_mine.shape),
            jnp.broadcast_to(r_low_high, (places // 2,) + r_low_high.shape).reshape(
                places, tok, n_k
            ),
        ],
        1,
    )
    got = exchange(sent.reshape(-1, n_s), ("dp", "row"))
    a_other = core(a_own)
    depth = a_own.shape[0]
    parts = []
    for cut in (slice(0, a_own.shape[1] // 8), slice(a_own.shape[1] // 8, None)):
        part = dot(a_own[:, cut], m_all[:depth], 0, 0)
        part = part + dot(a_other[:, cut], m_all[depth:], 0, 0)
        parts.append(part.astype(BF))
    got, first, *parts = lax.optimization_barrier((got, other_dp(parts[0]), *parts))
    got = got.reshape(n_dp, n_row, (n_dp + 1) * tok, n_s)
    source = d * (n_row // 2) + lax.axis_index("row") // 2
    r_piece = lax.dynamic_slice(got, (0, source, n_dp * tok, 0), (n_dp, 1, tok, n_k))
    r_piece = r_piece.reshape(n_dp * tok, n_k)
    v = lax.dynamic_slice(got, (d, 0, 0, 0), (1, n_row, n_dp * tok, n_s))
    v = v[0].transpose(1, 0, 2).reshape(n_dp * tok, n_row * n_s)

    v_cols = got.reshape(n_dp, 2, n_z // 2, (n_dp + 1) * tok, 2, n_w)
    v_cols = lax.dynamic_slice(
        v_cols,
        (0, 0, d * (n_z // 4), 0, 0, 0),
        (n_dp, 2, n_z // 4, n_dp * tok, 2, n_w),
    )
    v_cols = v_cols.transpose(2, 4, 1, 0, 3, 5).reshape(n_col, n_dp * tok, n_w)
    r_rep = jnp.broadcast_to(r_piece, (n_col,) + r_piece.shape)
    sent = jnp.concatenate([r_rep, v_cols], 2).reshape(-1, n_k + n_w)
    got = exchange(sent, "col")
    second = other_dp(parts[1])
    big_weight = jnp.concatenate([total(parts[0], first), total(parts[1], second)], 0)
    got, big_weight = lax.optimization_barrier((got, big_weight))
    grad_b = dot(x_t, got[:, :n_k], 1, 0)
    grad_a = dot(c_t, got[:, n_k:], 1, 0)

    low, high = v[:, :depth], v[:, depth:]
    v_own = jnp.where(core_id == 0, low, high)
    v_rest = jnp.where(core_id == 0, high, low)
    y_part = (dot(v_own, a_own, 1, 0) + dot(v_rest, a_other, 1, 0)).astype(BF)
    outputs = total(
        rows(y_part, d * tok, tok), other_dp(rows(y_part, (1 - d) * tok, tok))
    )

    return outputs, big_weight, grad_weight, grad_a, grad_b


def solution(mesh):
    return jax.shard_map(
        body,
        mesh=mesh,
        in_specs=(
            P("col", "row"),
            P("row", "col"),
            P("col", "row"),
            P("dp", "col"),
            P("dp", "row"),
        ),
        out_specs=(
            P(("dp", "col"), "row"),
            P("row", "col"),
            P("row", "col"),
            P("row", ("dp", "col")),
            P("col", ("dp", "row")),
        ),
        check_vma=False,
    )
```
